32 devices in a mesh: rep: 4 (over y, x), row: 2 (over core), col: 4 (over z).
Axes of the slice: x: 2, y: 2, z: 4, core: 2. Of those that a mesh axis runs over, the one named last changes fastest.
Arguments:
- acts: bfloat16 [4, 256, 5120], P('rep', None, 'row'), may hold values from -6 to 6
- grad_out: bfloat16 [4, 256, 13824], P('rep', None, 'col'), may hold values from -0.375 to 0.375
- momentum: bfloat16 [4, 5120, 13824], P('rep', 'row', 'col'), may hold values from -6 to 6
- q_basis: bfloat16 [640, 13824], P(None, 'col'), may hold values from -6 to 6
Outputs:
- momentum_next: bfloat16 [4, 5120, 13824], P('rep', 'row', 'col')
- q_next: bfloat16 [640, 13824], P('row', 'col')
- update: bfloat16 [5120, 13824], P('row', 'col')
The draws below stay inside these ranges and needn't reach their ends.
All inputs are finite; a program needn't handle non-finite values.
Results may differ from the reference program's by a relative error of at most 0.019.
Values may be sent and summed in bfloat16 or wider, within the bound.
A program may use at most 128 MiB of HBM per device.

```python
import jax
import jax.numpy as jnp
from jax import lax

D = 5120
FF = 13824
RANK = 640
TOK = 256
REPS = 4


def block_scale(rng, dims, pieces, low, high):
    def one(axis_at, blocks):
        draws = jax.random.uniform(jax.random.fold_in(jax.random.fold_in(rng, 6), axis_at), (blocks,), jnp.float32, low / len(pieces), high / len(pieces))
        return jnp.repeat(jnp.exp(draws), dims[axis_at] // blocks).reshape((-1,) + (1,) * (len(dims) - axis_at - 1))

    level = one(*pieces[0])
    for cut in pieces[1:]:
        level = level * one(*cut)
    return level


def centred(key, dims, spread, limit, shards=(), kind=jnp.bfloat16):
    drawn = spread * jax.random.normal(key, dims, jnp.float32)
    if shards:
        drawn = drawn * block_scale(key, dims, shards, -0.22, 0.18)
    return jnp.clip(drawn, -limit, limit).astype(kind)


def setup_inputs(seed: int = 0) -> dict:
    key_of = jax.random.split(jax.random.key(seed), 5)
    return {
        "acts": centred(key_of[0], (REPS, TOK, D), 1.0, 6.0, ((0, 4), (2, 2))),
        "grad_out": centred(key_of[1], (REPS, TOK, FF), TOK ** -0.5, 0.375, ((0, 4), (2, 4))),
        "momentum": centred(key_of[2], (REPS, D, FF), 1.0, 6.0, ((0, 4), (1, 2), (2, 4))),
        "q_basis": centred(key_of[3], (RANK, FF), 1.0, 6.0, ((1, 4),)),
    }


keep_factor = 0.6

def reference(acts, grad_out, momentum, q_basis):
    left = jnp.zeros((D, RANK), jnp.float32)
    boosted_all = []
    for replica in range(REPS):
        grad = jnp.dot(acts[replica].T.astype(jnp.float32), grad_out[replica].astype(jnp.float32), preferred_element_type=jnp.float32)
        boosted = (momentum[replica].astype(jnp.float32) + grad).astype(jnp.bfloat16)
        boosted_all.append(boosted)
        left = left + jnp.dot(boosted.astype(jnp.float32), q_basis.T.astype(jnp.float32), preferred_element_type=jnp.float32)
    gram = jnp.dot(left.T, left, precision=lax.Precision.HIGHEST)
    chol = jnp.linalg.cholesky(gram)
    ortho = lax.linalg.triangular_solve(chol, left, left_side=False, lower=True, transpose_a=True).astype(jnp.bfloat16)
    right_sum = jnp.zeros((RANK, FF), jnp.float32)
    for replica in range(REPS):
        right_sum = right_sum + jnp.dot(ortho.T.astype(jnp.float32), boosted_all[replica].astype(jnp.float32), preferred_element_type=jnp.float32)
    right = (right_sum * (1.0 / REPS)).astype(jnp.bfloat16)
    right_wide = right.astype(jnp.float32)
    msq = lax.optimization_barrier(jnp.mean(right_wide * right_wide, axis=1))
    q_full = (right_wide * lax.rsqrt(msq + 1e-06)[:, None]).astype(jnp.bfloat16)
    feedback = jnp.dot(ortho.astype(jnp.float32), right.astype(jnp.float32), preferred_element_type=jnp.float32)
    momentum_next = jnp.stack([(boosted_all[replica].astype(jnp.float32) - (1.0 - keep_factor) * feedback).astype(jnp.bfloat16) for replica in range(REPS)])
    update = (jnp.sqrt(jnp.float32(D) / RANK) * jnp.dot(ortho.astype(jnp.float32), q_full.astype(jnp.float32), preferred_element_type=jnp.float32)).astype(jnp.bfloat16)
    return (momentum_next, q_full, update)
```

```python
import functools

import jax
import jax.numpy as jnp
from jax import lax
from jax.experimental import pallas as pl
from jax.experimental.pallas import tpu as pltpu
from jax.sharding import PartitionSpec as P

BLOCK = 128
TILE = 8

keep_factor = 0.6


def dot_f32(a, b, dims):
    return lax.dot_general(
        a, b, (dims, ((), ())), precision=lax.Precision.HIGHEST, preferred_element_type=jnp.float32
    )


def block_factor(block):
    lane = lax.broadcasted_iota(jnp.int32, (1, BLOCK), 1)
    sub = lax.broadcasted_iota(jnp.int32, (TILE, 1), 0)
    tiles = [block[t * TILE : (t + 1) * TILE] for t in range(BLOCK // TILE)]
    for k in range(BLOCK):
        at, r = divmod(k, TILE)
        here = lane == k
        row = tiles[at][r : r + 1]
        scale = lax.rsqrt(jnp.broadcast_to(row[:, k : k + 1], (1, BLOCK)))
        done = jnp.where(here, 1.0, row) * scale
        used = done * scale
        tile = tiles[at]
        later = jnp.where(here, 0.0, tile) - tile[:, k : k + 1] * used
        tiles[at] = jnp.where(sub == r, done, jnp.where(sub > r, later, tile))
        for t in range(at + 1, len(tiles)):
            tile = tiles[t]
            tiles[t] = jnp.where(here, 0.0, tile) - tile[:, k : k + 1] * used
    whole = jnp.concatenate(tiles, axis=0)
    rows = lax.broadcasted_iota(jnp.int32, (BLOCK, BLOCK), 0)
    cols = lax.broadcasted_iota(jnp.int32, (BLOCK, BLOCK), 1)
    return jnp.where(rows >= cols, whole, 0.0)


def inverse_kernel(gram_ref, high_ref, low_ref, work):
    size = gram_ref.shape[0]
    work[...] = gram_ref[...]
    row_at = lax.broadcasted_iota(jnp.int32, (size, 1), 0)

    def step(j, carry):
        at = pl.ds(pl.multiple_of(j * BLOCK, BLOCK), BLOCK)
        factor = block_factor(work[at, at])
        panel = dot_f32(work[:, at], factor, ((1,), (1,)))
        panel = jnp.where(row_at >= (j + 1) * BLOCK, panel, 0.0)
        work[at, :] = dot_f32(factor, work[at, :], ((1,), (0,)))
        work[at, at] = factor
        rest = row_at >= (j + 1) * BLOCK
        work[:, at] = jnp.where(rest, 0.0, work[:, at])
        work[...] -= dot_f32(panel, work[at, :], ((1,), (0,)))
        return carry

    lax.fori_loop(0, size // BLOCK, step, 0)
    rows = lax.broadcasted_iota(jnp.int32, (size, size), 0)
    cols = lax.broadcasted_iota(jnp.int32, (size, size), 1)
    inverse = jnp.where(rows >= cols, work[...], 0.0)
    high = inverse.astype(jnp.bfloat16)
    high_ref[...] = high
    low_ref[...] = (inverse - high.astype(jnp.float32)).astype(jnp.bfloat16)


def inverse_factor(gram):
    size = gram.shape[0]
    return pl.pallas_call(
        inverse_kernel,
        out_shape=[jax.ShapeDtypeStruct((size, size), jnp.bfloat16)] * 2,
        in_specs=[pl.BlockSpec(memory_space=pltpu.VMEM)],
        out_specs=[pl.BlockSpec(memory_space=pltpu.VMEM)] * 2,
        scratch_shapes=[pltpu.VMEM((size, size), jnp.float32)],
        compiler_params=pltpu.CompilerParams(vmem_limit_bytes=24 * 1024 * 1024),
        cost_estimate=pl.CostEstimate(
            flops=60_000_000_000, bytes_accessed=6 * size * size, transcendentals=size
        ),
        name="inverse_factor",
    )(gram)


def matmul(a, b, dims):
    return lax.dot_general(a, b, (dims, ((), ())), preferred_element_type=jnp.float32)


def shards(acts, grad_out, momentum, q_basis):
    grad = matmul(acts[0], grad_out[0], ((0,), (0,)))
    boosted = (momentum[0].astype(jnp.float32) + grad).astype(jnp.bfloat16)
    partial_value = matmul(boosted, q_basis, ((1,), (1,))).astype(jnp.bfloat16)
    piece = lax.psum_scatter(partial_value, "rep", scatter_dimension=0, tiled=True)
    piece = lax.psum_scatter(piece, "col", scatter_dimension=0, tiled=True)
    piece = lax.all_gather(piece, "col", axis=0, tiled=True)
    left = lax.all_gather(piece, "rep", axis=0, tiled=True)
    gram_part, left = lax.optimization_barrier((matmul(left, left, ((0,), (0,))), left))
    gram = lax.psum(gram_part, "row")
    replicas = lax.axis_size("rep")
    moved = matmul(left, boosted, ((0,), (0,))).astype(jnp.bfloat16)
    gram, moved = lax.optimization_barrier((gram, moved))
    moved = lax.psum(moved, ("row", "rep"))
    high, low = inverse_factor(gram)
    right_sum = matmul(high, moved, ((1,), (0,))) + matmul(low, moved, ((1,), (0,)))
    right = (right_sum * (1.0 / replicas)).astype(jnp.bfloat16)
    ortho = (matmul(left, high, ((1,), (1,))) + matmul(left, low, ((1,), (1,)))).astype(
        jnp.bfloat16
    )
    right_wide = right.astype(jnp.float32)
    columns_all = right.shape[1] * lax.axis_size("col")
    squares = lax.psum(jnp.sum(right_wide * right_wide, axis=1), "col")
    feedback = matmul(ortho, right, ((1,), (0,)))
    momentum_next = (boosted.astype(jnp.float32) - (1.0 - keep_factor) * feedback).astype(
        jnp.bfloat16
    )[None]
    msq = squares / columns_all
    q_full = (right_wide * lax.rsqrt(msq + 1e-06)[:, None]).astype(jnp.bfloat16)
    rank = q_basis.shape[0]
    block = rank // lax.axis_size("row")
    q_next = lax.dynamic_slice_in_dim(q_full, lax.axis_index("row") * block, block, 0)
    width_all = boosted.shape[0] * lax.axis_size("row")
    update = (
        jnp.sqrt(jnp.float32(width_all) / rank) * matmul(ortho, q_full, ((1,), (0,)))
    ).astype(jnp.bfloat16)
    return (momentum_next, q_next, update)


def solution(mesh):
    in_specs = (
        P("rep", None, "row"),
        P("rep", None, "col"),
        P("rep", "row", "col"),
        P(None, "col"),
    )
    out_specs = (P("rep", "row", "col"), P("row", "col"), P("row", "col"))
    return jax.shard_map(shards, mesh=mesh, in_specs=in_specs, out_specs=out_specs, check_vma=False)
```
